32 devices in a mesh: slab: 16 (over z, y, x), panel: 2 (over core).
Axes of the slice: x: 2, y: 2, z: 4, core: 2. Of those that a mesh axis runs over, the one named last changes fastest.
Arguments:
- weights: bfloat16 [5120, 8192], P('slab', 'panel'), may hold values from -6 to 6
- gain: float32 [8192], replicated, may hold values from 0.1 to 1.9
- rotation: float32 [8192, 8192], P('panel', 'slab'), may hold values from -0.0625 to 0.0625
- tokens: bfloat16 [512, 8192], P(None, 'slab'), may hold values from -1400 to 1400
Outputs:
- served: bfloat16 [2, 2560, 8192], P('panel', 'slab')
- qkv: bfloat16 [512, 5120], P('slab', 'panel')
The draws below stay inside these ranges and needn't reach their ends.
All inputs are finite; a program needn't handle non-finite values.
Results may differ from the reference program's by a relative error of at most 0.0049.
Values may be sent and summed in bfloat16 or wider, within the bound.
No kernel may reach another device: no remote copies, remote signals or barrier semaphores. Data moves between devices by JAX's collectives and lax.ppermute only.
A program may use at most 192 MiB of HBM per device.

```python
import math
import jax
import jax.numpy as jnp
from jax import lax

D = 8192
ROWS = 5120
TOKENS = 512
N_PANEL = 2


def draw_tokens(key, part):
    key = jax.random.fold_in(key, 7)
    base_key, row_key, rough_key = jax.random.split(key, 3)
    ramp = jnp.power(10.0, jnp.arange(D, dtype=jnp.float32) / D)[None, :]
    rough = jax.random.uniform(rough_key, (1, D), jnp.float32, 0.7, 1.4)
    base = jax.random.normal(base_key, (TOKENS, D), jnp.float32)
    row_scale = jnp.exp(jax.random.uniform(row_key, (TOKENS, 1), jnp.float32, 0.0, math.log(10.0)))
    base = jnp.clip(base, -6.0, 6.0)
    return (base * row_scale * ramp * rough).astype(jnp.bfloat16)


def levels(key, shape, pieces, least, largest):
    factor_of = 1.0
    for position, shards_of in pieces:
        steps = jax.random.uniform(jax.random.fold_in(jax.random.fold_in(key, 6), position), (shards_of,), jnp.float32, least / len(pieces), largest / len(pieces))
        factor_of = factor_of * jnp.repeat(jnp.exp(steps), shape[position] // shards_of).reshape((-1,) + (1,) * (len(shape) - 1 - position))
    return factor_of


def normal_values(own_key, dims, spread, limit, shards=(), kind=jnp.bfloat16):
    values = spread * jax.random.normal(own_key, dims, jnp.float32)
    if shards:
        values = values * levels(own_key, dims, shards, -0.22, 0.18)
    return jnp.clip(values, -limit, limit).astype(kind)


def setup_inputs(seed: int = 0) -> dict:
    seeds = jax.random.split(jax.random.key(seed), 5)
    weights = normal_values(seeds[0], (ROWS, D), 1.0, 6.0, ((0, 16), (1, 2)))
    gain = jnp.clip(1.0 + 0.18 * jax.random.normal(seeds[1], (D,), jnp.float32), 0.1, 1.9)
    rotation = normal_values(seeds[2], (D, D), D ** -0.5, 0.0625, ((0, 2), (1, 16)), jnp.float32)
    tokens = draw_tokens(jax.random.fold_in(seeds[4], 71), 0)
    return {"weights": weights, "gain": gain, "rotation": rotation, "tokens": tokens}


EPS = 1e-05

def reference(weights, gain, rotation, tokens):
    scaled = weights.astype(jnp.float32) * gain[None, :]
    folded = jnp.dot(scaled, rotation, precision=lax.Precision.HIGHEST, preferred_element_type=jnp.float32)
    exported = folded.astype(jnp.bfloat16)
    product = lax.dot_general(tokens, exported, (((1,), (1,)), ((), ())), preferred_element_type=jnp.float32)
    widened = tokens.astype(jnp.float32)
    meansq = lax.optimization_barrier(jnp.sum(widened * widened, axis=1)) / D
    qkv = (product * lax.rsqrt(meansq + EPS)[:, None] / math.sqrt(D)).astype(jnp.bfloat16)
    served = exported.reshape(N_PANEL, ROWS // N_PANEL, D)
    return (served, qkv)
```

```python
import functools
import math

import jax
import jax.numpy as jnp
from jax import lax
from jax.experimental import pallas as pl
from jax.experimental.pallas import tpu as pltpu
from jax.sharding import PartitionSpec as P

D = 8192


EPS = 1e-05


def general_shards(weights, gain, rotation, tokens):
    width_rows = rotation.shape[0]
    gain_block = lax.dynamic_slice_in_dim(gain, lax.axis_index("panel") * width_rows, width_rows, 0)
    partial_value = jnp.dot(
        lax.all_gather(weights, "slab", axis=0, tiled=True),
        (rotation * gain_block[:, None]).astype(jnp.bfloat16),
        preferred_element_type=jnp.float32,
    )
    folded = lax.psum_scatter(partial_value, "panel", scatter_dimension=0, tiled=True)
    exported = folded.astype(jnp.bfloat16)
    product = lax.dot_general(
        tokens, exported, (((1,), (1,)), ((), ())), preferred_element_type=jnp.float32
    )
    widened = tokens.astype(jnp.float32)
    squares = jnp.sum(widened * widened, axis=1)
    whole, whole_squares = lax.psum((product, squares), "slab")
    own_count = tokens.shape[0] // lax.axis_size("slab")
    first_token = lax.axis_index("slab") * own_count
    total = lax.dynamic_slice_in_dim(whole, first_token, own_count, 0)
    square_sum = lax.dynamic_slice_in_dim(whole_squares, first_token, own_count, 0)
    meansq = square_sum / D
    qkv = (total * lax.rsqrt(meansq + EPS)[:, None] / math.sqrt(D)).astype(jnp.bfloat16)
    whole_rows = lax.all_to_all(exported, "slab", split_axis=0, concat_axis=1, tiled=True)
    return (whole_rows[None], qkv)


CHIPS = [(x, y, z) for z in range(4) for y in range(2) for x in range(2)]
NEAR = [(dx, dy) for dy in range(2) for dx in range(2)]


def slab_of(x, y, z):
    return z * 4 + y * 2 + x


def move(value, dx=0, dy=0, dz=0):
    pairs = [(slab_of(x, y, z), slab_of(x ^ dx, y ^ dy, z ^ dz)) for x, y, z in CHIPS]
    return lax.ppermute(value, "slab", pairs)


def swap_cores(value):
    return lax.ppermute(value, "panel", [(0, 1), (1, 0)])


def send_rows(value, f, dx, dy):
    pairs = []
    for x, y, z in CHIPS:
        for q in range(2):
            target = slab_of(q, x ^ dx, 2 * (z % 2) + (y ^ dy)) * 2 + ((z // 2) ^ f)
            pairs.append((slab_of(x, y, z) * 2 + q, target))
    return lax.ppermute(value, ("slab", "panel"), pairs)


def tie(values, *others):
    return lax.optimization_barrier((values, others))[0]


def fold_kernel(plan, turn_plan, n_chunks, given, *refs):
    n_in = 1 + max(max(p[0] for p in plan), max(p[0] for turn in turn_plan for p in turn))
    ins, before, refs = refs[:n_in], refs[n_in : n_in + given], refs[n_in + given :]
    outs, (together, rows, held, sums, sems) = refs[:-5], refs[-5:]
    n_rows, depth = rows.shape
    width = held.shape[2]
    size = n_rows // len(outs)
    step = depth // n_chunks
    copies, index = [], 0
    for c in range(n_chunks):
        group = []
        for k, turn in enumerate(turn_plan):
            for p, first, count, begin in turn:
                low, high = max(begin, c * step), min(begin + count, (c + 1) * step)
                if low < high:
                    source = ins[p].at[pl.ds(first + low - begin, high - low)]
                    group.append(pltpu.make_async_copy(source, held.at[k, pl.ds(low, high - low)], sems.at[index]))
                    index += 1
        for p, first, count, place in plan:
            columns = pl.ds(c * step, step)
            source = ins[p].at[pl.ds(first, count), columns]
            group.append(pltpu.make_async_copy(source, rows.at[pl.ds(place, count), columns], sems.at[index]))
            index += 1
        copies.append(group)
    shift = before[0].shape[1] if given else 0
    for group in copies:
        for copy in group:
            copy.start()
    for c, group in enumerate(copies):
        for copy in group:
            copy.wait()
        if given and not c:
            together[:, :shift] = before[0][...]
            for i, out in enumerate(outs):
                out[:, :shift] = before[0][i * size : (i + 1) * size]
        for k in range(len(turn_plan)):
            columns = slice(k * width, (k + 1) * width)
            value = jnp.dot(
                rows[:, c * step : (c + 1) * step],
                held[k, c * step : (c + 1) * step],
                preferred_element_type=jnp.float32,
            )
            if c:
                value = value + sums[:, columns]
            if c < n_chunks - 1:
                sums[:, columns] = value
            else:
                value = value.astype(jnp.bfloat16)
                columns = slice(shift + k * width, shift + (k + 1) * width)
                together[:, columns] = value
                for i, out in enumerate(outs):
                    out[:, columns] = value[i * size : (i + 1) * size]


def fold(blocks, turns, before=()):
    arrays, plan, turn_plan, place = [], [], [], 0

    def operand(value):
        for i, other in enumerate(arrays):
            if other is value:
                return i
        arrays.append(value)
        return len(arrays) - 1

    for block in blocks:
        for value, first, count in block:
            plan.append((operand(value), first, count, place))
            place += count
    for turn in turns:
        begins = [sum(count for _, _, count in turn[:i]) for i in range(len(turn))]
        turn_plan.append([(operand(v), first, count, begin) for (v, first, count), begin in zip(turn, begins)])
    depth, width = blocks[0][0][0].shape[1], turns[0][0][0].shape[1]
    n, t, n_chunks = len(blocks), len(turns), 8
    all_width = t * width + sum(value.shape[1] for value in before)
    n_copies = n_chunks * (len(plan) + 2 * sum(len(turn) for turn in turn_plan))
    out = pl.pallas_call(
        functools.partial(fold_kernel, plan, turn_plan, n_chunks, len(before)),
        out_shape=[jax.ShapeDtypeStruct((place // n, all_width), jnp.bfloat16)] * n
        + [jax.ShapeDtypeStruct((place, all_width), jnp.bfloat16)],
        in_specs=[pl.BlockSpec(memory_space=pltpu.HBM)] * len(arrays)
        + [pl.BlockSpec(memory_space=pltpu.VMEM)] * len(before),
        out_specs=[pl.BlockSpec(memory_space=pltpu.VMEM)] * (n + 1),
        scratch_shapes=[
            pltpu.VMEM((place, depth), jnp.bfloat16),
            pltpu.VMEM((t, depth, width), jnp.bfloat16),
            pltpu.VMEM((place, t * width), jnp.float32),
            pltpu.SemaphoreType.DMA((n_copies,)),
        ],
        compiler_params=pltpu.CompilerParams(vmem_limit_bytes=60 * 1024 * 1024),
        cost_estimate=pl.CostEstimate(flops=1024, bytes_accessed=1024, transcendentals=0),
    )(*arrays, *before)
    return out[:-1], out[-1]


def place_kernel(plan, width, *refs):
    ins, out, sems = refs[:-2], refs[-2], refs[-1]
    slab, core = lax.axis_index("slab"), lax.axis_index("panel")
    x, y, z = slab % 2, (slab // 2) % 2, slab // 4
    copies = []
    for ref, (f, dx, dy) in zip(ins, plan):
        for j in range(2):
            z_source = (core + f) % 2 * 2 + (z // 2 + j) % 2
            source = z_source * 4 + (z + dy) % 2 * 2 + (y + dx) % 2
            target = out.at[:, pl.ds(pl.multiple_of(source * width, width), width)]
            copies.append(pltpu.make_async_copy(ref.at[:, pl.ds(j * width, width)], target, sems.at[len(copies)]))
    for copy in copies:
        copy.start()
    for copy in copies:
        copy.wait()


def whole_rows(pieces, width):
    plan = [key for key, _ in pieces]
    return pl.pallas_call(
        functools.partial(place_kernel, plan, width),
        out_shape=jax.ShapeDtypeStruct((pieces[0][1].shape[0], D), jnp.bfloat16),
        in_specs=[pl.BlockSpec(memory_space=pl.ANY)] * len(pieces),
        out_specs=pl.BlockSpec(memory_space=pltpu.VMEM),
        scratch_shapes=[pltpu.SemaphoreType.DMA((2 * len(plan),))],
        cost_estimate=pl.CostEstimate(flops=1024, bytes_accessed=1024, transcendentals=0),
    )(*[value for _, value in pieces])


def shards(weights, gain, rotation, tokens):
    slab, core = lax.axis_index("slab"), lax.axis_index("panel")
    x, y, z = slab % 2, (slab // 2) % 2, slab // 4
    z_hi, z_lo = z // 2, z % 2
    depth, width = rotation.shape
    half = weights.shape[0] // 2
    low = half // 2
    n_tokens = tokens.shape[0]
    own_count = n_tokens // 16

    def split(value, axis, bit):
        size = value.shape[axis] // 2
        return [lax.dynamic_slice_in_dim(value, b * size, size, axis) for b in (bit, 1 - bit)]

    mine, others = split(weights, 0, core)
    rows = jnp.concatenate([mine, swap_cores(others)], axis=1)

    ordered = tokens.reshape(2, 2, 2, 2, own_count, width).transpose(3, 2, 0, 1, 4, 5).reshape(n_tokens, width)
    part = split(ordered, 0, core)[0]

    gain_block = lax.dynamic_slice_in_dim(gain, core * depth, depth, 0)
    turn = (rotation * gain_block[:, None]).astype(jnp.bfloat16)
    cuts = [0, 3 * depth // 16, depth // 2, depth]
    pieces = [turn[i:j] for i, j in zip(cuts, cuts[1:])]

    def spread(values, f):
        return [send_rows(value, f, *key) for value, key in zip(values, NEAR)]

    def check(exported):
        return lax.dot_general(exported, checks, (((1,), (1,)), ((), ())), preferred_element_type=jnp.float32)

    def three_terms(values):
        terms = []
        for _ in range(3):
            terms.append(values.astype(jnp.bfloat16).astype(jnp.float32))
            values = values - terms[-1]
        return jnp.concatenate([jnp.stack(terms), jnp.zeros((13, values.shape[0]), jnp.float32)])

    def quarter(value, dx, dy):
        size = n_tokens // 4
        return lax.dynamic_slice_in_dim(value, ((x ^ dx) * 2 + (y ^ dy)) * size, size, 1)

    def plane(values):
        got = {}
        for d in NEAR:
            value = [quarter(v, *d) for v in values]
            got[d] = move(jnp.concatenate([v.astype(jnp.bfloat16) for v in value]), *d) if any(d) else value
        return got

    def total(sums):
        value = sums[0].reshape(2, 2, half, -1)
        for (dx, dy), blocks in zip(NEAR[1:], sums[1:]):
            blocks = blocks.astype(jnp.float32).reshape(2, 2, half, -1)
            blocks = blocks[::-1] if dy else blocks
            value = value + (blocks[:, ::-1] if dx else blocks)
        return value.reshape(4 * half, -1)

    near_x, near_y, far_low, piece_a, turn_swapped = tie(
        (
            move(rows, dx=1),
            move(rows, dy=1),
            move(rows[:low], dz=2),
            move(jnp.concatenate([pieces[0], part]), dz=1),
            swap_cores(turn),
        )
    )
    by_x, by_y, far_high, piece_b, swapped_a = tie(
        (
            move(jnp.concatenate([near_y[low:], far_low]), dx=1),
            move(jnp.concatenate([near_x[:low], far_low]), dy=1),
            move(rows[low:], dz=2),
            move(pieces[1], dz=1),
            swap_cores(piece_a),
        )
    )
    first = pieces[0].shape[0]
    part, swapped = piece_a[first:], swapped_a[first:]
    ordered_other = jnp.concatenate([jnp.where(core == 0, part, swapped), jnp.where(core == 0, swapped, part)])
    checks = jnp.concatenate([ordered, ordered_other], axis=1)
    widened = checks.astype(jnp.float32)
    squares = jnp.sum(widened * widened, axis=1)
    terms = three_terms(squares)
    cut = 3 * low // 5
    own_turn = [(turn, 0, depth), (turn_swapped, 0, depth)]
    near = [
        [(rows, 0, half)],
        [(near_x, 0, half)],
        [(near_y, 0, half)],
        [(by_y, 0, low), (by_x, 0, low)],
    ]
    by_x3, by_y3, piece_c, swapped_b, near_own, checks, terms = tie(
        (
            move(jnp.concatenate([far_high, by_y[low + cut :]]), dx=1),
            move(jnp.concatenate([far_high, by_x[low : low + cut]]), dy=1),
            move(pieces[2], dz=1),
            swap_cores(piece_b),
            fold(near, [own_turn]),
            checks,
            terms,
        )
    )
    swapped_c = swap_cores(piece_c)
    arrived = [piece_a, piece_b, piece_c, swapped_a, swapped_b, swapped_c]
    turn_other = [(v, 0, p.shape[0]) for v, p in zip(arrived, pieces + pieces)]
    by_y4, by_x4, near_rows = tie(
        (
            move(by_x3[: low - cut], dy=1),
            move(by_y3[low - cut : low], dx=1),
            fold(near, [turn_other], [near_own[1]]),
        )
    )
    far = [
        [(far_low, 0, low), (far_high, 0, low)],
        [(by_x, low, low), (by_x3, 0, low)],
        [(by_y, low, low), (by_y3, 0, low)],
        [(by_y3, low, cut), (by_x3, low, low - cut), (by_y4, 0, low - cut), (by_x4, 0, cut)],
    ]
    received_near, far_rows = tie((spread(near_rows[0], 0), fold(far, [own_turn, turn_other])))
    sums = plane([check(near_rows[1]), check(far_rows[1]), terms])
    received_far, sums = tie((spread(far_rows[0], 1), sums))
    placed = [((f,) + d, v) for f, values in enumerate((received_near, received_far)) for d, v in zip(NEAR, values)]
    served = whole_rows(placed, width)

    rows_near, rows_far, own_squares = sums[0, 0]
    kept = [rows_near, rows_far]
    for f in range(2):
        kept[f] = total([kept[f]] + [sums[d][4 * half * f : 4 * half * (f + 1)] for d in NEAR[1:]])
    own_squares = own_squares + sum(sums[d][8 * half :].astype(jnp.float32) for d in NEAR[1:])
    own_squares = jnp.sum(own_squares, axis=0)
    near_keep, near_give = split(kept[0], 1, z_hi)
    far_keep, far_give = split(kept[1], 1, z_hi)
    keep_squares, give_squares = split(own_squares, 0, z_hi)
    given = jnp.concatenate([near_give, far_give, three_terms(give_squares)]).astype(jnp.bfloat16)
    got = move(given, dz=2).astype(jnp.float32)
    own_scale = lax.rsqrt((keep_squares + jnp.sum(got[8 * half :], axis=0)) / D + EPS)
    shape = (2, 2, half, 2 * own_count)
    near_keep = (near_keep + got[4 * half : 8 * half]).reshape(shape)
    far_keep = (far_keep + got[: 4 * half]).reshape(shape)
    result = (jnp.stack([near_keep, far_keep]) * own_scale / math.sqrt(D)).astype(jnp.bfloat16)
    keep = lax.dynamic_index_in_dim(result, z_hi ^ core, 0, keepdims=False)
    got = swap_cores(lax.dynamic_index_in_dim(result, z_hi ^ 1 ^ core, 0, keepdims=False))
    both = jnp.stack([keep, got], axis=2)
    keep = lax.dynamic_slice_in_dim(both, z_lo * own_count, own_count, 4)
    got = move(lax.dynamic_slice_in_dim(both, (1 - z_lo) * own_count, own_count, 4), dz=1)
    whole = jnp.stack([keep, got]).reshape(16, half, own_count)
    flip = ((z_lo * 2 + y) * 2 + x) * 2 + core
    whole = jnp.take(whole, jnp.arange(16) ^ flip, axis=0)
    qkv = whole.reshape(16 * half, own_count).T
    return (served[None], qkv)


def solution(mesh):
    placed = (P("slab", "panel"), P(), P("panel", "slab"), P(None, "slab"))
    small = mesh.shape["slab"] == 16 and mesh.shape["panel"] == 2
    return jax.shard_map(
        shards if small else general_shards,
        mesh=mesh,
        in_specs=placed,
        out_specs=(P("panel", "slab", None), P("slab", "panel")),
        check_vma=False,
    )
```

```python
import functools
import math

import jax
import jax.numpy as jnp
from jax import lax
from jax.experimental import pallas as pl
from jax.experimental.pallas import tpu as pltpu
from jax.sharding import PartitionSpec as P

D = 8192


EPS = 1e-05


def general_shards(weights, gain, rotation, tokens):
    width_rows = rotation.shape[0]
    gain_block = lax.dynamic_slice_in_dim(gain, lax.axis_index("panel") * width_rows, width_rows, 0)
    partial_value = jnp.dot(
        lax.all_gather(weights, "slab", axis=0, tiled=True),
        (rotation * gain_block[:, None]).astype(jnp.bfloat16),
        preferred_element_type=jnp.float32,
    )
    folded = lax.psum_scatter(partial_value, "panel", scatter_dimension=0, tiled=True)
    exported = folded.astype(jnp.bfloat16)
    product = lax.dot_general(
        tokens, exported, (((1,), (1,)), ((), ())), preferred_element_type=jnp.float32
    )
    widened = tokens.astype(jnp.float32)
    squares = jnp.sum(widened * widened, axis=1)
    whole, whole_squares = lax.psum((product, squares), "slab")
    own_count = tokens.shape[0] // lax.axis_size("slab")
    first_token = lax.axis_index("slab") * own_count
    total = lax.dynamic_slice_in_dim(whole, first_token, own_count, 0)
    square_sum = lax.dynamic_slice_in_dim(whole_squares, first_token, own_count, 0)
    meansq = square_sum / D
    qkv = (total * lax.rsqrt(meansq + EPS)[:, None] / math.sqrt(D)).astype(jnp.bfloat16)
    whole_rows = lax.all_to_all(exported, "slab", split_axis=0, concat_axis=1, tiled=True)
    return (whole_rows[None], qkv)


CHIPS = [(x, y, z) for z in range(4) for y in range(2) for x in range(2)]
NEAR = [(dx, dy) for dy in range(2) for dx in range(2)]


def slab_of(x, y, z):
    return z * 4 + y * 2 + x


def move(value, dx=0, dy=0, dz=0):
    pairs = [(slab_of(x, y, z), slab_of(x ^ dx, y ^ dy, z ^ dz)) for x, y, z in CHIPS]
    return lax.ppermute(value, "slab", pairs)


def swap_cores(value):
    return lax.ppermute(value, "panel", [(0, 1), (1, 0)])


def send_rows(value, f, dx, dy):
    pairs = []
    for x, y, z in CHIPS:
        for q in range(2):
            target = slab_of(q, x ^ dx, 2 * (z % 2) + (y ^ dy)) * 2 + ((z // 2) ^ f)
            pairs.append((slab_of(x, y, z) * 2 + q, target))
    return lax.ppermute(value, ("slab", "panel"), pairs)


def tie(values, *others):
    return lax.optimization_barrier((values, others))[0]


def fold_kernel(plan, turn_plan, n_chunks, keys, ready_keys, given, *refs):
    n, n_ready = len(keys), len(ready_keys)
    n_in = 1 + max(max(p[0] for p in plan), max(p[0] for turn in turn_plan for p in turn))
    ins, refs = refs[:n_in], refs[n_in:]
    before, ready, refs = refs[:given], refs[given : given + n_ready], refs[given + n_ready :]
    outs, together, (rows, held, sums, sems) = refs[:n], refs[n:-4], refs[-4:]
    n_rows, depth = rows.shape
    width = held.shape[2]
    size = n_rows // n
    step = depth // n_chunks
    slab = lax.axis_index("slab")
    x, y = slab % 2, (slab // 2) % 2

    def slot(key):
        return pl.ds(pl.multiple_of(((y + key[1]) % 2 * 2 + (x + key[0]) % 2) * size, 32), size)

    copies, index = [], 0
    for c in range(n_chunks):
        group = []
        for k, turn in enumerate(turn_plan):
            for p, first, count, begin in turn:
                low, high = max(begin, c * step), min(begin + count, (c + 1) * step)
                if low < high:
                    source = ins[p].at[pl.ds(first + low - begin, high - low)]
                    group.append(pltpu.make_async_copy(source, held.at[k, pl.ds(low, high - low)], sems.at[index]))
                    index += 1
        for p, first, count, place in plan:
            columns = pl.ds(c * step, step)
            source = ins[p].at[pl.ds(first, count), columns]
            group.append(pltpu.make_async_copy(source, rows.at[pl.ds(place, count), columns], sems.at[index]))
            index += 1
        copies.append(group)
    for group in copies[:2]:
        for copy in group:
            copy.start()
    shift = before[0].shape[1] if given else 0
    for value, key in zip(ready, ready_keys):
        together[0][slot(key), :] = value[...]
    for c, group in enumerate(copies):
        for copy in group:
            copy.wait()
        for copy in copies[c + 2] if c + 2 < n_chunks else []:
            copy.start()
        if given and not c:
            for i, out in enumerate(outs):
                out[:, :shift] = before[i][...]
        for k in range(len(turn_plan)):
            columns = slice(k * width, (k + 1) * width)
            value = jnp.dot(
                rows[:, c * step : (c + 1) * step],
                held[k, c * step : (c + 1) * step],
                preferred_element_type=jnp.float32,
            )
            if c:
                value = value + sums[:, columns]
            if c < n_chunks - 1:
                sums[:, columns] = value
            else:
                value = value.astype(jnp.bfloat16)
                for i, out in enumerate(outs):
                    out[:, shift + k * width : shift + (k + 1) * width] = value[i * size : (i + 1) * size]
    for out, key in zip(outs, keys):
        if key is not None:
            together[0][slot(key), :] = out[...]


def fold(blocks, turns, before=(), keys=None, ready=()):
    arrays, plan, turn_plan, place = [], [], [], 0

    def operand(value):
        for i, other in enumerate(arrays):
            if other is value:
                return i
        arrays.append(value)
        return len(arrays) - 1

    for block in blocks:
        for value, first, count in block:
            plan.append((operand(value), first, count, place))
            place += count
    for turn in turns:
        begins = [sum(count for _, _, count in turn[:i]) for i in range(len(turn))]
        turn_plan.append([(operand(v), first, count, begin) for (v, first, count), begin in zip(turn, begins)])
    depth, width = blocks[0][0][0].shape[1], turns[0][0][0].shape[1]
    n, t, n_chunks = len(blocks), len(turns), 4
    size, all_width = place // n, t * width + (before[0].shape[1] if before else 0)
    n_copies = n_chunks * (len(plan) + 2 * sum(len(turn) for turn in turn_plan))
    shapes = [jax.ShapeDtypeStruct((size, all_width), jnp.bfloat16)] * n
    if keys:
        shapes.append(jax.ShapeDtypeStruct((4 * size, all_width), jnp.bfloat16))
    ready_values, ready_keys = [v for v, _ in ready], [k for _, k in ready]
    out = pl.pallas_call(
        functools.partial(
            fold_kernel, plan, turn_plan, n_chunks, keys or [None] * n, ready_keys, len(before)
        ),
        out_shape=shapes,
        in_specs=[pl.BlockSpec(memory_space=pltpu.HBM)] * len(arrays)
        + [pl.BlockSpec(memory_space=pltpu.VMEM)] * (len(before) + len(ready)),
        out_specs=[pl.BlockSpec(memory_space=pltpu.VMEM)] * len(shapes),
        scratch_shapes=[
            pltpu.VMEM((place, depth), jnp.bfloat16),
            pltpu.VMEM((t, depth, width), jnp.bfloat16),
            pltpu.VMEM((place, t * width), jnp.float32),
            pltpu.SemaphoreType.DMA((n_copies,)),
        ],
        compiler_params=pltpu.CompilerParams(vmem_limit_bytes=60 * 1024 * 1024),
        cost_estimate=pl.CostEstimate(flops=1024, bytes_accessed=1024, transcendentals=0),
    )(*arrays, *before, *ready_values)
    return (out[:-1], out[-1]) if keys else out


def place_kernel(plan, width, *refs):
    ins, out, sems = refs[:-2], refs[-2], refs[-1]
    slab, core = lax.axis_index("slab"), lax.axis_index("panel")
    x, y, z = slab % 2, (slab // 2) % 2, slab // 4
    copies = []
    for ref, (f, dx, dy) in zip(ins, plan):
        for j in range(2):
            z_source = (core + f) % 2 * 2 + (z // 2 + j) % 2
            source = z_source * 4 + (z + dy) % 2 * 2 + (y + dx) % 2
            target = out.at[:, pl.ds(pl.multiple_of(source * width, width), width)]
            copies.append(pltpu.make_async_copy(ref.at[:, pl.ds(j * width, width)], target, sems.at[len(copies)]))
    for copy in copies:
        copy.start()
    for copy in copies:
        copy.wait()


def whole_rows(pieces, width):
    plan = [key for key, _ in pieces]
    return pl.pallas_call(
        functools.partial(place_kernel, plan, width),
        out_shape=jax.ShapeDtypeStruct((pieces[0][1].shape[0], D), jnp.bfloat16),
        in_specs=[pl.BlockSpec(memory_space=pl.ANY)] * len(pieces),
        out_specs=pl.BlockSpec(memory_space=pltpu.VMEM),
        scratch_shapes=[pltpu.SemaphoreType.DMA((2 * len(plan),))],
        cost_estimate=pl.CostEstimate(flops=1024, bytes_accessed=1024, transcendentals=0),
    )(*[value for _, value in pieces])


def shards(weights, gain, rotation, tokens):
    slab, core = lax.axis_index("slab"), lax.axis_index("panel")
    x, y, z = slab % 2, (slab // 2) % 2, slab // 4
    z_hi, z_lo = z // 2, z % 2
    depth, width = rotation.shape
    half = weights.shape[0] // 2
    low = half // 2
    n_tokens = tokens.shape[0]
    own_count = n_tokens // 16

    def split(value, axis, bit):
        size = value.shape[axis] // 2
        return [lax.dynamic_slice_in_dim(value, b * size, size, axis) for b in (bit, 1 - bit)]

    mine, others = split(weights, 0, core)
    rows = jnp.concatenate([mine, swap_cores(others)], axis=1)

    ordered = tokens.reshape(2, 2, 2, 2, own_count, width).transpose(3, 2, 0, 1, 4, 5).reshape(n_tokens, width)
    part = split(ordered, 0, core)[0]

    gain_block = lax.dynamic_slice_in_dim(gain, core * depth, depth, 0)[:, None]
    cuts = [0, 7 * depth // 32, 18 * depth // 32, depth]
    first_piece = (rotation[: cuts[1]] * gain_block[: cuts[1]]).astype(jnp.bfloat16)
    rotation, gain_block = tie((rotation, gain_block), rows)
    turn = (rotation * gain_block).astype(jnp.bfloat16)
    pieces = [first_piece] + [turn[i:j] for i, j in zip(cuts[1:], cuts[2:])]

    def spread(values, f, keys=NEAR):
        return [send_rows(value, f, *key) for value, key in zip(values, keys)]

    def check(exported):
        return lax.dot_general(checks, exported, (((1,), (1,)), ((), ())), preferred_element_type=jnp.float32)

    def three_terms(values):
        terms = []
        for _ in range(3):
            terms.append(values.astype(jnp.bfloat16).astype(jnp.float32))
            values = values - terms[-1]
        return jnp.pad(jnp.stack(terms, axis=1), ((0, 0), (0, 125)))

    def halve(values, squares, bit, dx=0, dy=0, dz=0):
        keep, give = split(values, 0, bit)
        if dz:
            give = jnp.roll(give, give.shape[1] // 2, axis=1)
        keep_squares, give_squares = split(squares, 0, bit)
        got = move(jnp.concatenate([give, three_terms(give_squares)], axis=1).astype(jnp.bfloat16), dx, dy, dz)
        got = got.astype(jnp.float32)
        n = values.shape[1]
        return keep + got[:, :n], keep_squares + jnp.sum(got[:, n:], axis=1)

    near_x, near_y, far_low, piece_a, pieces = tie(
        (
            move(rows, dx=1),
            move(rows, dy=1),
            move(rows[:low], dz=2),
            move(jnp.concatenate([pieces[0], part]), dz=1),
            pieces,
        )
    )
    by_x, by_y, far_high, piece_b, turn_swapped, last_piece = tie(
        (
            move(jnp.concatenate([near_y[low:], far_low]), dx=1),
            move(jnp.concatenate([near_x[:low], far_low]), dy=1),
            move(rows[low:], dz=2),
            move(pieces[1], dz=1),
            swap_cores(turn),
            pieces[2],
        )
    )
    cut = 3 * low // 5
    own_turn = [(turn, 0, depth), (turn_swapped, 0, depth)]
    early = [
        [(rows, 0, half)],
        [(near_x, 0, half)],
        [(near_y, 0, half)],
        [(by_y, 0, low), (by_x, 0, low)],
        [(far_low, 0, low), (far_high, 0, low)],
    ]
    early_own, piece_c = tie((fold(early, [own_turn]), move(last_piece, dz=1)))
    by_x3, by_y3, swapped_a, swapped_b, swapped_c = tie(
        (
            move(jnp.concatenate([far_high, by_y[2 * low - cut :]]), dx=1),
            move(jnp.concatenate([far_high, by_x[low : low + cut]]), dy=1),
            swap_cores(piece_a),
            swap_cores(piece_b),
            swap_cores(piece_c),
        )
    )
    first = pieces[0].shape[0]
    part, swapped = piece_a[first:], swapped_a[first:]
    ordered_other = jnp.concatenate([jnp.where(core == 0, part, swapped), jnp.where(core == 0, swapped, part)])
    checks = jnp.concatenate([ordered, ordered_other], axis=1)
    widened = checks.astype(jnp.float32)
    squares = jnp.sum(widened * widened, axis=1)
    arrived = [piece_a, piece_b, piece_c, swapped_a, swapped_b, swapped_c]
    turn_other = [(v, 0, p.shape[0]) for v, p in zip(arrived, pieces + pieces)]
    by_y4, by_x4, (early_rows, near_rows) = tie(
        (
            move(by_x3[: low - cut], dy=1),
            move(by_y3[low - cut : low], dx=1),
            fold(early, [turn_other], early_own, NEAR + [None]),
        )
    )
    late = [
        [(by_x, low, low), (by_x3, 0, low)],
        [(by_y, low, low), (by_y3, 0, low)],
        [(by_y3, low, cut), (by_x3, 2 * cut, low - cut), (by_y4, 0, low - cut), (by_x4, 0, cut)],
    ]
    received_near, received_far, (late_rows, far_rows) = tie(
        (
            spread(early_rows[:4], 0),
            spread(early_rows[4:], 1),
            fold(late, [own_turn, turn_other], (), NEAR[1:], [(early_rows[4], NEAR[0])]),
        )
    )
    products = jnp.concatenate([check(near_rows), check(far_rows)], axis=1)

    def quarter(value, dx, dy):
        size = n_tokens // 4
        return lax.dynamic_slice_in_dim(value, ((x ^ dx) * 2 + (y ^ dy)) * size, size, 0)

    def to_send(d):
        terms = three_terms(quarter(squares, *d))
        return jnp.concatenate([quarter(products, *d).astype(jnp.bfloat16), terms.astype(jnp.bfloat16)], axis=1)

    parts, received = tie(([move(to_send(d), *d) for d in NEAR[1:]], spread(late_rows[:2], 1, NEAR[1:])))
    received_far = received_far + received
    got = sum(v.astype(jnp.float32) for v in parts)
    sums = quarter(products, 0, 0) + got[:, : 8 * half]
    squares = quarter(squares, 0, 0) + jnp.sum(got[:, 8 * half :], axis=1)
    sums, squares, received = tie(halve(sums, squares, z_hi, dz=2) + (spread(late_rows[2:], 1, NEAR[3:]),))
    received_far = received_far + received
    placed = [((f,) + d, v) for f, values in enumerate((received_near, received_far)) for d, v in zip(NEAR, values)]
    served = whole_rows(placed, width)

    result = (sums * lax.rsqrt(squares / D + EPS)[:, None] / math.sqrt(D)).astype(jnp.bfloat16)
    keep, give = split(result, 1, z_hi ^ core)
    got = swap_cores(give)
    both = jnp.concatenate([jnp.where(core == 0, keep, got), jnp.where(core == 0, got, keep)], axis=1)
    keep, give = split(both, 0, z_lo)
    got = move(give, dz=1)
    whole = jnp.stack([jnp.where(z_lo == 0, keep, got), jnp.where(z_lo == 0, got, keep)], axis=1)
    qkv = whole.reshape(own_count, 2, 2, 4, half).transpose(0, 1, 3, 2, 4).reshape(own_count, 16 * half)
    return (served[None], qkv)


def solution(mesh):
    placed = (P("slab", "panel"), P(), P("panel", "slab"), P(None, "slab"))
    small = mesh.shape["slab"] == 16 and mesh.shape["panel"] == 2
    return jax.shard_map(
        shards if small else general_shards,
        mesh=mesh,
        in_specs=placed,
        out_specs=(P("panel", "slab", None), P("slab", "panel")),
        check_vma=False,
    )
```

```python
import functools
import math

import jax
import jax.numpy as jnp
from jax import lax
from jax.experimental import pallas as pl
from jax.experimental.pallas import tpu as pltpu
from jax.sharding import PartitionSpec as P

D = 8192


EPS = 1e-05


def general_shards(weights, gain, rotation, tokens):
    width_rows = rotation.shape[0]
    gain_block = lax.dynamic_slice_in_dim(gain, lax.axis_index("panel") * width_rows, width_rows, 0)
    partial_value = jnp.dot(
        lax.all_gather(weights, "slab", axis=0, tiled=True),
        (rotation * gain_block[:, None]).astype(jnp.bfloat16),
        preferred_element_type=jnp.float32,
    )
    folded = lax.psum_scatter(partial_value, "panel", scatter_dimension=0, tiled=True)
    exported = folded.astype(jnp.bfloat16)
    product = lax.dot_general(
        tokens, exported, (((1,), (1,)), ((), ())), preferred_element_type=jnp.float32
    )
    widened = tokens.astype(jnp.float32)
    squares = jnp.sum(widened * widened, axis=1)
    whole, whole_squares = lax.psum((product, squares), "slab")
    own_count = tokens.shape[0] // lax.axis_size("slab")
    first_token = lax.axis_index("slab") * own_count
    total = lax.dynamic_slice_in_dim(whole, first_token, own_count, 0)
    square_sum = lax.dynamic_slice_in_dim(whole_squares, first_token, own_count, 0)
    meansq = square_sum / D
    qkv = (total * lax.rsqrt(meansq + EPS)[:, None] / math.sqrt(D)).astype(jnp.bfloat16)
    whole_rows = lax.all_to_all(exported, "slab", split_axis=0, concat_axis=1, tiled=True)
    return (whole_rows[None], qkv)


CHIPS = [(x, y, z) for z in range(4) for y in range(2) for x in range(2)]
NEAR = [(dx, dy) for dy in range(2) for dx in range(2)]


def slab_of(x, y, z):
    return z * 4 + y * 2 + x


def move(value, dx=0, dy=0, dz=0):
    pairs = [(slab_of(x, y, z), slab_of(x ^ dx, y ^ dy, z ^ dz)) for x, y, z in CHIPS]
    return lax.ppermute(value, "slab", pairs)


def swap_cores(value):
    return lax.ppermute(value, "panel", [(0, 1), (1, 0)])


def send_rows(value, f, dx, dy):
    pairs = []
    for x, y, z in CHIPS:
        for q in range(2):
            target = slab_of(q, x ^ dx, 2 * (z % 2) + (y ^ dy)) * 2 + ((z // 2) ^ f)
            pairs.append((slab_of(x, y, z) * 2 + q, target))
    return lax.ppermute(value, ("slab", "panel"), pairs)


def tie(values, *others):
    return lax.optimization_barrier((values, others))[0]


def fold_kernel(plan, turn_plan, steps, n_done, keys, ready_keys, n_begun, given, *refs):
    n, n_ready = len(keys), len(ready_keys)
    n_in = 1 + max(max(p[0] for p in plan), max(p[0] for turn in turn_plan for p in turn))
    ins, refs = refs[:n_in], refs[n_in:]
    begun, refs = refs[:n_begun], refs[n_begun:]
    before, ready, refs = refs[:given], refs[given : given + n_ready], refs[given + n_ready :]
    outs, more, (rows, held, sums, sems) = refs[:n], refs[n:-4], refs[-4:]
    n_rows, _ = rows.shape
    width = held.shape[2]
    size = n_rows // n
    slab = lax.axis_index("slab")
    x, y = slab % 2, (slab // 2) % 2

    def slot(key):
        return pl.ds(pl.multiple_of(((y + key[1]) % 2 * 2 + (x + key[0]) % 2) * size, 32), size)

    copies, index, loaded = [], 0, set()
    for k, begin, end in steps:
        group = []
        for p, first, count, place in turn_plan[k]:
            low, high = max(place, begin), min(place + count, end)
            if low < high:
                source = ins[p].at[pl.ds(first + low - place, high - low)]
                group.append(pltpu.make_async_copy(source, held.at[k, pl.ds(low, high - low)], sems.at[index]))
                index += 1
        if not any(low <= begin and end <= high for low, high in loaded):
            loaded.add((begin, end))
            loaded.update([(low, end) for low, high in loaded if high == begin])
            for p, first, count, place in plan:
                columns = pl.ds(begin, end - begin)
                source = ins[p].at[pl.ds(first, count), columns]
                group.append(pltpu.make_async_copy(source, rows.at[pl.ds(place, count), columns], sems.at[index]))
                index += 1
        copies.append(group)
    for group in copies[:2]:
        for copy in group:
            copy.start()
    shift = before[0].shape[1] if given else 0
    for value, key in zip(ready, ready_keys):
        more[0][slot(key), :] = value[...]
    last = {k: i for i, (k, _, _) in enumerate(steps)}
    started = set(range(n_begun))
    for i, (k, begin, end) in enumerate(steps):
        for copy in copies[i]:
            copy.wait()
        for copy in copies[i + 2] if i + 2 < len(steps) else []:
            copy.start()
        if given and not i:
            for out, value in zip(outs, before):
                out[:, :shift] = value[...]
        columns = slice(k * width, (k + 1) * width)
        value = jnp.dot(rows[:, begin:end], held[k, begin:end], preferred_element_type=jnp.float32)
        if k in started:
            value = value + (begun[k][...] if k < n_begun and (k, 0) not in started else sums[:, columns])
            started.add((k, 0))
        started.add(k)
        if i < last[k]:
            sums[:, columns] = value
            started.add((k, 0))
        elif k >= n_done:
            more[-1][...] = value
        else:
            value = value.astype(jnp.bfloat16)
            for j, out in enumerate(outs):
                out[:, shift + k * width : shift + (k + 1) * width] = value[j * size : (j + 1) * size]
    for out, key in zip(outs, keys):
        if key is not None:
            more[0][slot(key), :] = out[...]


def fold(blocks, turns, steps, before=(), keys=None, ready=(), begun=(), n_done=None):
    arrays, plan, turn_plan, place = [], [], [], 0

    def operand(value):
        for i, other in enumerate(arrays):
            if other is value:
                return i
        arrays.append(value)
        return len(arrays) - 1

    for block in blocks:
        for value, first, count in block:
            plan.append((operand(value), first, count, place))
            place += count
    for turn in turns:
        turn_plan.append([(operand(v), first, count, begin) for v, first, count, begin in turn])
    depth, width = blocks[0][0][0].shape[1], turns[0][0][0].shape[1]
    n, t = len(blocks), len(turns)
    n_done = t if n_done is None else n_done
    size, all_width = place // n, n_done * width + (before[0].shape[1] if before else 0)
    n_copies = len(steps) * (len(plan) + sum(len(turn) for turn in turn_plan))
    shapes = [jax.ShapeDtypeStruct((size, all_width), jnp.bfloat16)] * n
    if keys:
        shapes.append(jax.ShapeDtypeStruct((4 * size, all_width), jnp.bfloat16))
    if n_done < t:
        shapes.append(jax.ShapeDtypeStruct((place, width), jnp.float32))
    ready_values, ready_keys = [v for v, _ in ready], [k for _, k in ready]
    out = pl.pallas_call(
        functools.partial(
            fold_kernel, plan, turn_plan, steps, n_done, keys or [None] * n, ready_keys, len(begun), len(before)
        ),
        out_shape=shapes,
        in_specs=[pl.BlockSpec(memory_space=pltpu.HBM)] * len(arrays)
        + [pl.BlockSpec(memory_space=pltpu.VMEM)] * (len(begun) + len(before) + len(ready)),
        out_specs=[pl.BlockSpec(memory_space=pltpu.VMEM)] * len(shapes),
        scratch_shapes=[
            pltpu.VMEM((place, depth), jnp.bfloat16),
            pltpu.VMEM((t, depth, width), jnp.bfloat16),
            pltpu.VMEM((place, t * width), jnp.float32),
            pltpu.SemaphoreType.DMA((n_copies,)),
        ],
        compiler_params=pltpu.CompilerParams(vmem_limit_bytes=60 * 1024 * 1024),
        cost_estimate=pl.CostEstimate(flops=1024, bytes_accessed=1024, transcendentals=0),
    )(*arrays, *begun, *before, *ready_values)
    return out[:n], out[n:]


def place_kernel(plan, width, *refs):
    ins, out, sems = refs[:-2], refs[-2], refs[-1]
    slab, core = lax.axis_index("slab"), lax.axis_index("panel")
    x, y, z = slab % 2, (slab // 2) % 2, slab // 4
    copies = []
    for ref, (f, dx, dy) in zip(ins, plan):
        for j in range(2):
            z_source = (core + f) % 2 * 2 + (z // 2 + j) % 2
            source = z_source * 4 + (z + dy) % 2 * 2 + (y + dx) % 2
            target = out.at[:, pl.ds(pl.multiple_of(source * width, width), width)]
            copies.append(pltpu.make_async_copy(ref.at[:, pl.ds(j * width, width)], target, sems.at[len(copies)]))
    for copy in copies:
        copy.start()
    for copy in copies:
        copy.wait()


def whole_rows(pieces, width):
    plan = [key for key, _ in pieces]
    return pl.pallas_call(
        functools.partial(place_kernel, plan, width),
        out_shape=jax.ShapeDtypeStruct((pieces[0][1].shape[0], D), jnp.bfloat16),
        in_specs=[pl.BlockSpec(memory_space=pl.ANY)] * len(pieces),
        out_specs=pl.BlockSpec(memory_space=pltpu.VMEM),
        scratch_shapes=[pltpu.SemaphoreType.DMA((2 * len(plan),))],
        cost_estimate=pl.CostEstimate(flops=1024, bytes_accessed=1024, transcendentals=0),
    )(*[value for _, value in pieces])


def shards(weights, gain, rotation, tokens):
    slab, core = lax.axis_index("slab"), lax.axis_index("panel")
    x, y, z = slab % 2, (slab // 2) % 2, slab // 4
    z_hi, z_lo = z // 2, z % 2
    depth, width = rotation.shape
    half = weights.shape[0] // 2
    low = half // 2
    n_tokens = tokens.shape[0]
    own_count = n_tokens // 16

    def split(value, axis, bit):
        size = value.shape[axis] // 2
        return [lax.dynamic_slice_in_dim(value, b * size, size, axis) for b in (bit, 1 - bit)]

    mine, others = split(weights, 0, core)
    rows = jnp.concatenate([mine, swap_cores(others)], axis=1)

    ordered = tokens.reshape(2, 2, 2, 2, own_count, width).transpose(3, 2, 0, 1, 4, 5).reshape(n_tokens, width)
    part = split(ordered, 0, core)[0]

    gain_block = lax.dynamic_slice_in_dim(gain, core * depth, depth, 0)[:, None]
    cuts = [0, 7 * depth // 32, 18 * depth // 32, depth]
    first_piece = (rotation[: cuts[1]] * gain_block[: cuts[1]]).astype(jnp.bfloat16)
    rotation, gain_block = tie((rotation, gain_block), rows)
    turn = (rotation * gain_block).astype(jnp.bfloat16)
    pieces = [first_piece] + [turn[i:j] for i, j in zip(cuts[1:], cuts[2:])]

    def spread(values, f, keys=NEAR):
        return [send_rows(value, f, *key) for value, key in zip(values, keys)]

    def check(exported):
        return lax.dot_general(checks, exported, (((1,), (1,)), ((), ())), preferred_element_type=jnp.float32)

    def three_terms(values):
        terms = []
        for _ in range(3):
            terms.append(values.astype(jnp.bfloat16).astype(jnp.float32))
            values = values - terms[-1]
        return jnp.pad(jnp.stack(terms, axis=1), ((0, 0), (0, 125)))

    def halve(values, squares, bit, dx=0, dy=0, dz=0):
        keep, give = split(values, 0, bit)
        if dz:
            give = jnp.roll(give, give.shape[1] // 2, axis=1)
        keep_squares, give_squares = split(squares, 0, bit)
        got = move(jnp.concatenate([give, three_terms(give_squares)], axis=1).astype(jnp.bfloat16), dx, dy, dz)
        got = got.astype(jnp.float32)
        n = values.shape[1]
        return keep + got[:, :n], keep_squares + jnp.sum(got[:, n:], axis=1)

    near_x, near_y, far_low, piece_a, pieces = tie(
        (
            move(rows, dx=1),
            move(rows, dy=1),
            move(rows[:low], dz=2),
            move(jnp.concatenate([pieces[0], part]), dz=1),
            pieces,
        )
    )
    by_x, by_y, far_high, piece_b, turn_swapped, last_piece = tie(
        (
            move(jnp.concatenate([near_y[low:], far_low]), dx=1),
            move(jnp.concatenate([near_x[:low], far_low]), dy=1),
            move(rows[low:], dz=2),
            move(pieces[1], dz=1),
            swap_cores(turn),
            pieces[2],
        )
    )
    cut = 3 * low // 5
    own_turn = [(turn, 0, depth, 0), (turn_swapped, 0, depth, depth)]
    quarters = [(i * depth // 2, (i + 1) * depth // 2) for i in range(4)]
    swapped_a, swapped_b = swap_cores(piece_a), swap_cores(piece_b)
    places = cuts[:3] + [depth + cut for cut in cuts[:3]]
    other_turn = [(v, 0, p.shape[0], q) for v, p, q in zip([piece_a, piece_b, swapped_a, swapped_b], (pieces[:2]) * 2, [places[i] for i in (0, 1, 3, 4)])]
    early = [
        [(rows, 0, half)],
        [(near_x, 0, half)],
        [(near_y, 0, half)],
        [(by_y, 0, low), (by_x, 0, low)],
        [(far_low, 0, low), (far_high, 0, low)],
    ]
    (early_own, early_sums), piece_c = tie(
        (
            fold(
                early,
                [own_turn, other_turn],
                [(0,) + q for q in quarters] + [(1, 0, cuts[2]), (1, depth, depth + cuts[2])],
                n_done=1,
            ),
            move(last_piece, dz=1),
        )
    )
    swapped_c = swap_cores(piece_c)
    last_turn = [(piece_c, 0, depth - cuts[2], cuts[2]), (swapped_c, 0, depth - cuts[2], depth + cuts[2])]
    by_x3, by_y3, swapped_a, swapped_b, swapped_c, (early_rows, (near_rows,)) = tie(
        (
            move(jnp.concatenate([far_high, by_y[2 * low - cut :]]), dx=1),
            move(jnp.concatenate([far_high, by_x[low : low + cut]]), dy=1),
            swapped_a,
            swapped_b,
            swapped_c,
            fold(
                early,
                [last_turn],
                [(0, cuts[2], depth), (0, depth + cuts[2], 2 * depth)],
                early_own,
                NEAR + [None],
                begun=early_sums,
            ),
        )
    )
    first = pieces[0].shape[0]
    part, swapped = piece_a[first:], swapped_a[first:]
    ordered_other = jnp.concatenate([jnp.where(core == 0, part, swapped), jnp.where(core == 0, swapped, part)])
    checks = jnp.concatenate([ordered, ordered_other], axis=1)
    widened = checks.astype(jnp.float32)
    squares = jnp.sum(widened * widened, axis=1)
    arrived = [piece_a, piece_b, piece_c, swapped_a, swapped_b, swapped_c]
    other_turn = [(v, 0, p.shape[0], q) for v, p, q in zip(arrived, pieces + pieces, places)]
    by_y4, by_x4, received_first, early_rows = tie(
        (
            move(by_x3[: low - cut], dy=1),
            move(by_y3[low - cut : low], dx=1),
            spread(early_rows[:1], 0),
            early_rows,
        )
    )
    late = [
        [(by_x, low, low), (by_x3, 0, low)],
        [(by_y, low, low), (by_y3, 0, low)],
        [(by_y3, low, cut), (by_x3, 2 * cut, low - cut), (by_y4, 0, low - cut), (by_x4, 0, cut)],
    ]
    received_near, received_far, (late_rows, (far_rows,)) = tie(
        (
            spread(early_rows[1:4], 0, NEAR[1:]),
            spread(early_rows[4:], 1),
            fold(
                late,
                [own_turn, other_turn],
                [(k,) + q for q in quarters for k in range(2)],
                (),
                NEAR[1:],
                [(early_rows[4], NEAR[0])],
            ),
        )
    )
    received_near = received_first + received_near
    products = jnp.concatenate([check(near_rows), check(far_rows)], axis=1)

    def quarter(value, dx, dy):
        size = n_tokens // 4
        return lax.dynamic_slice_in_dim(value, ((x ^ dx) * 2 + (y ^ dy)) * size, size, 0)

    def to_send(d):
        terms = three_terms(quarter(squares, *d))
        return jnp.concatenate([quarter(products, *d).astype(jnp.bfloat16), terms.astype(jnp.bfloat16)], axis=1)

    parts, received = tie(([move(to_send(d), *d) for d in NEAR[1:]], spread(late_rows[:2], 1, NEAR[1:])))
    received_far = received_far + received
    got = sum(v.astype(jnp.float32) for v in parts)
    sums = quarter(products, 0, 0) + got[:, : 8 * half]
    squares = quarter(squares, 0, 0) + jnp.sum(got[:, 8 * half :], axis=1)
    sums, squares, received = tie(halve(sums, squares, z_hi, dz=2) + (spread(late_rows[2:], 1, NEAR[3:]),))
    received_far = received_far + received
    placed = [((f,) + d, v) for f, values in enumerate((received_near, received_far)) for d, v in zip(NEAR, values)]
    served = whole_rows(placed, width)

    result = (sums * lax.rsqrt(squares / D + EPS)[:, None] / math.sqrt(D)).astype(jnp.bfloat16)
    keep, give = split(result, 1, z_hi ^ core)
    got = swap_cores(give)
    both = jnp.concatenate([jnp.where(core == 0, keep, got), jnp.where(core == 0, got, keep)], axis=1)
    keep, give = split(both, 0, z_lo)
    got = move(give, dz=1)
    whole = jnp.stack([jnp.where(z_lo == 0, keep, got), jnp.where(z_lo == 0, got, keep)], axis=1)
    qkv = whole.reshape(own_count, 2, 2, 4, half).transpose(0, 1, 3, 2, 4).reshape(own_count, 16 * half)
    return (served[None], qkv)


def solution(mesh):
    placed = (P("slab", "panel"), P(), P("panel", "slab"), P(None, "slab"))
    small = mesh.shape["slab"] == 16 and mesh.shape["panel"] == 2
    return jax.shard_map(
        shards if small else general_shards,
        mesh=mesh,
        in_specs=placed,
        out_specs=(P("panel", "slab", None), P("slab", "panel")),
        check_vma=False,
    )
```

```python
import functools
import math

import jax
import jax.numpy as jnp
from jax import lax
from jax.experimental import pallas as pl
from jax.experimental.pallas import tpu as pltpu
from jax.sharding import PartitionSpec as P

D = 8192


EPS = 1e-05


def general_shards(weights, gain, rotation, tokens):
    width_rows = rotation.shape[0]
    gain_block = lax.dynamic_slice_in_dim(gain, lax.axis_index("panel") * width_rows, width_rows, 0)
    partial_value = jnp.dot(
        lax.all_gather(weights, "slab", axis=0, tiled=True),
        (rotation * gain_block[:, None]).astype(jnp.bfloat16),
        preferred_element_type=jnp.float32,
    )
    folded = lax.psum_scatter(partial_value, "panel", scatter_dimension=0, tiled=True)
    exported = folded.astype(jnp.bfloat16)
    product = lax.dot_general(
        tokens, exported, (((1,), (1,)), ((), ())), preferred_element_type=jnp.float32
    )
    widened = tokens.astype(jnp.float32)
    squares = jnp.sum(widened * widened, axis=1)
    whole, whole_squares = lax.psum((product, squares), "slab")
    own_count = tokens.shape[0] // lax.axis_size("slab")
    first_token = lax.axis_index("slab") * own_count
    total = lax.dynamic_slice_in_dim(whole, first_token, own_count, 0)
    square_sum = lax.dynamic_slice_in_dim(whole_squares, first_token, own_count, 0)
    meansq = square_sum / D
    qkv = (total * lax.rsqrt(meansq + EPS)[:, None] / math.sqrt(D)).astype(jnp.bfloat16)
    whole_rows = lax.all_to_all(exported, "slab", split_axis=0, concat_axis=1, tiled=True)
    return (whole_rows[None], qkv)


CHIPS = [(x, y, z) for z in range(4) for y in range(2) for x in range(2)]
NEAR = [(dx, dy) for dy in range(2) for dx in range(2)]


def slab_of(x, y, z):
    return z * 4 + y * 2 + x


def move(value, dx=0, dy=0, dz=0):
    pairs = [(slab_of(x, y, z), slab_of(x ^ dx, y ^ dy, z ^ dz)) for x, y, z in CHIPS]
    return lax.ppermute(value, "slab", pairs)


def swap_cores(value):
    return lax.ppermute(value, "panel", [(0, 1), (1, 0)])


def send_rows(value, f, dx, dy):
    pairs = []
    for x, y, z in CHIPS:
        for q in range(2):
            target = slab_of(q, x ^ dx, 2 * (z % 2) + (y ^ dy)) * 2 + ((z // 2) ^ f)
            pairs.append((slab_of(x, y, z) * 2 + q, target))
    return lax.ppermute(value, ("slab", "panel"), pairs)


def tie(values, *others):
    return lax.optimization_barrier((values, others))[0]


def fold_kernel(plan, turn_plan, steps, n_done, keys, ready_keys, n_begun, given, *refs):
    n, n_ready = len(keys), len(ready_keys)
    n_in = 1 + max(max(p[0] for p in plan), max(p[0] for turn in turn_plan for p in turn))
    ins, refs = refs[:n_in], refs[n_in:]
    begun, refs = refs[:n_begun], refs[n_begun:]
    before, ready, refs = refs[:given], refs[given : given + n_ready], refs[given + n_ready :]
    outs, more, (rows, held, sums, sems) = refs[:n], refs[n:-4], refs[-4:]
    n_rows, _ = rows.shape
    width = held.shape[2]
    size = n_rows // n
    slab = lax.axis_index("slab")
    x, y = slab % 2, (slab // 2) % 2

    def slot(key):
        return pl.ds(pl.multiple_of(((y + key[1]) % 2 * 2 + (x + key[0]) % 2) * size, 32), size)

    copies, index, loaded = [], 0, set()
    for k, begin, end in steps:
        group = []
        for p, first, count, place in turn_plan[k]:
            low, high = max(place, begin), min(place + count, end)
            if low < high:
                source = ins[p].at[pl.ds(first + low - place, high - low)]
                group.append(pltpu.make_async_copy(source, held.at[k, pl.ds(low, high - low)], sems.at[index]))
                index += 1
        if not any(low <= begin and end <= high for low, high in loaded):
            loaded.add((begin, end))
            loaded.update([(low, end) for low, high in loaded if high == begin])
            for p, first, count, place in plan:
                columns = pl.ds(begin, end - begin)
                source = ins[p].at[pl.ds(first, count), columns]
                group.append(pltpu.make_async_copy(source, rows.at[pl.ds(place, count), columns], sems.at[index]))
                index += 1
        copies.append(group)
    for group in copies[:2]:
        for copy in group:
            copy.start()
    shift = before[0].shape[1] if given else 0
    for value, key in zip(ready, ready_keys):
        more[0][slot(key), :] = value[...]
    last = {k: i for i, (k, _, _) in enumerate(steps)}
    started = set(range(n_begun))
    for i, (k, begin, end) in enumerate(steps):
        for copy in copies[i]:
            copy.wait()
        for copy in copies[i + 2] if i + 2 < len(steps) else []:
            copy.start()
        if given and not i:
            for out, value in zip(outs, before):
                out[:, :shift] = value[...]
        columns = slice(k * width, (k + 1) * width)
        value = jnp.dot(rows[:, begin:end], held[k, begin:end], preferred_element_type=jnp.float32)
        if k in started:
            value = value + (begun[k][...] if k < n_begun and (k, 0) not in started else sums[:, columns])
            started.add((k, 0))
        started.add(k)
        if i < last[k]:
            sums[:, columns] = value
            started.add((k, 0))
        elif k >= n_done:
            more[-1][...] = value
        else:
            value = value.astype(jnp.bfloat16)
            for j, out in enumerate(outs):
                out[:, shift + k * width : shift + (k + 1) * width] = value[j * size : (j + 1) * size]
    for out, key in zip(outs, keys):
        if key is not None:
            more[0][slot(key), :] = out[...]


def fold(blocks, turns, steps, before=(), keys=None, ready=(), begun=(), n_done=None):
    arrays, plan, turn_plan, place = [], [], [], 0

    def operand(value):
        for i, other in enumerate(arrays):
            if other is value:
                return i
        arrays.append(value)
        return len(arrays) - 1

    for block in blocks:
        for value, first, count in block:
            plan.append((operand(value), first, count, place))
            place += count
    for turn in turns:
        turn_plan.append([(operand(v), first, count, begin) for v, first, count, begin in turn])
    depth, width = blocks[0][0][0].shape[1], turns[0][0][0].shape[1]
    n, t = len(blocks), len(turns)
    n_done = t if n_done is None else n_done
    size, all_width = place // n, n_done * width + (before[0].shape[1] if before else 0)
    n_copies = len(steps) * (len(plan) + sum(len(turn) for turn in turn_plan))
    shapes = [jax.ShapeDtypeStruct((size, all_width), jnp.bfloat16)] * n
    if keys:
        shapes.append(jax.ShapeDtypeStruct((4 * size, all_width), jnp.bfloat16))
    if n_done < t:
        shapes.append(jax.ShapeDtypeStruct((place, width), jnp.float32))
    ready_values, ready_keys = [v for v, _ in ready], [k for _, k in ready]
    out = pl.pallas_call(
        functools.partial(
            fold_kernel, plan, turn_plan, steps, n_done, keys or [None] * n, ready_keys, len(begun), len(before)
        ),
        out_shape=shapes,
        in_specs=[pl.BlockSpec(memory_space=pltpu.HBM)] * len(arrays)
        + [pl.BlockSpec(memory_space=pltpu.VMEM)] * (len(begun) + len(before) + len(ready)),
        out_specs=[pl.BlockSpec(memory_space=pltpu.VMEM)] * len(shapes),
        scratch_shapes=[
            pltpu.VMEM((place, depth), jnp.bfloat16),
            pltpu.VMEM((t, depth, width), jnp.bfloat16),
            pltpu.VMEM((place, t * width), jnp.float32),
            pltpu.SemaphoreType.DMA((n_copies,)),
        ],
        compiler_params=pltpu.CompilerParams(vmem_limit_bytes=60 * 1024 * 1024),
        cost_estimate=pl.CostEstimate(flops=1024, bytes_accessed=1024, transcendentals=0),
    )(*arrays, *begun, *before, *ready_values)
    return out[:n], out[n:]


def place_kernel(plan, width, *refs):
    ins, out, sems = refs[:-2], refs[-2], refs[-1]
    slab, core = lax.axis_index("slab"), lax.axis_index("panel")
    x, y, z = slab % 2, (slab // 2) % 2, slab // 4
    copies = []
    for ref, (f, dx, dy) in zip(ins, plan):
        for j in range(2):
            z_source = (core + f) % 2 * 2 + (z // 2 + j) % 2
            source = z_source * 4 + (z + dy) % 2 * 2 + (y + dx) % 2
            target = out.at[:, pl.ds(pl.multiple_of(source * width, width), width)]
            copies.append(pltpu.make_async_copy(ref.at[:, pl.ds(j * width, width)], target, sems.at[len(copies)]))
    for copy in copies:
        copy.start()
    for copy in copies:
        copy.wait()


def whole_rows(pieces, width):
    plan = [key for key, _ in pieces]
    return pl.pallas_call(
        functools.partial(place_kernel, plan, width),
        out_shape=jax.ShapeDtypeStruct((pieces[0][1].shape[0], D), jnp.bfloat16),
        in_specs=[pl.BlockSpec(memory_space=pl.ANY)] * len(pieces),
        out_specs=pl.BlockSpec(memory_space=pltpu.VMEM),
        scratch_shapes=[pltpu.SemaphoreType.DMA((2 * len(plan),))],
        cost_estimate=pl.CostEstimate(flops=1024, bytes_accessed=1024, transcendentals=0),
    )(*[value for _, value in pieces])


def shards(weights, gain, rotation, tokens):
    slab, core = lax.axis_index("slab"), lax.axis_index("panel")
    x, y, z = slab % 2, (slab // 2) % 2, slab // 4
    z_hi, z_lo = z // 2, z % 2
    depth, width = rotation.shape
    half = weights.shape[0] // 2
    low = half // 2
    n_tokens = tokens.shape[0]
    own_count = n_tokens // 16

    def split(value, axis, bit):
        size = value.shape[axis] // 2
        return [lax.dynamic_slice_in_dim(value, b * size, size, axis) for b in (bit, 1 - bit)]

    mine, others = split(weights, 0, core)
    rows = jnp.concatenate([mine, swap_cores(others)], axis=1)

    ordered = tokens.reshape(2, 2, 2, 2, own_count, width).transpose(3, 2, 0, 1, 4, 5).reshape(n_tokens, width)
    part = split(ordered, 0, core)[0]

    gain_block = lax.dynamic_slice_in_dim(gain, core * depth, depth, 0)[:, None]
    cuts = [0, 7 * depth // 32, 18 * depth // 32, depth]
    first_piece = (rotation[: cuts[1]] * gain_block[: cuts[1]]).astype(jnp.bfloat16)
    rotation, gain_block = tie((rotation, gain_block), rows)
    turn = (rotation * gain_block).astype(jnp.bfloat16)
    pieces = [first_piece] + [turn[i:j] for i, j in zip(cuts[1:], cuts[2:])]

    def spread(values, f, keys=NEAR):
        return [send_rows(value, f, *key) for value, key in zip(values, keys)]

    def check(exported):
        return lax.dot_general(checks, exported, (((1,), (1,)), ((), ())), preferred_element_type=jnp.float32)

    def three_terms(values):
        terms = []
        for _ in range(3):
            terms.append(values.astype(jnp.bfloat16).astype(jnp.float32))
            values = values - terms[-1]
        return jnp.pad(jnp.stack(terms, axis=1), ((0, 0), (0, 125)))

    def halve(values, squares, bit, dx=0, dy=0, dz=0):
        keep, give = split(values, 0, bit)
        if dz:
            give = jnp.roll(give, give.shape[1] // 2, axis=1)
        keep_squares, give_squares = split(squares, 0, bit)
        got = move(jnp.concatenate([give, three_terms(give_squares)], axis=1).astype(jnp.bfloat16), dx, dy, dz)
        got = got.astype(jnp.float32)
        n = values.shape[1]
        return keep + got[:, :n], keep_squares + jnp.sum(got[:, n:], axis=1)

    near_x, near_y, far_low, piece_a, pieces = tie(
        (
            move(rows, dx=1),
            move(rows, dy=1),
            move(rows[:low], dz=2),
            move(jnp.concatenate([pieces[0], part]), dz=1),
            pieces,
        )
    )
    by_x, by_y, far_high, piece_b, turn_swapped, last_piece = tie(
        (
            move(jnp.concatenate([near_y[low:], far_low]), dx=1),
            move(jnp.concatenate([near_x[:low], far_low]), dy=1),
            move(rows[low:], dz=2),
            move(pieces[1], dz=1),
            swap_cores(turn),
            pieces[2],
        )
    )
    cut = 3 * low // 5
    own_turn = [(turn, 0, depth, 0), (turn_swapped, 0, depth, depth)]
    quarters = [(i * depth // 2, (i + 1) * depth // 2) for i in range(4)]
    swapped_a, swapped_b = swap_cores(piece_a), swap_cores(piece_b)
    places = cuts[:3] + [depth + cut for cut in cuts[:3]]
    other_turn = [(v, 0, p.shape[0], q) for v, p, q in zip([piece_a, piece_b, swapped_a, swapped_b], (pieces[:2]) * 2, [places[i] for i in (0, 1, 3, 4)])]
    early = [
        [(rows, 0, half)],
        [(near_x, 0, half)],
        [(near_y, 0, half)],
        [(by_y, 0, low), (by_x, 0, low)],
        [(far_low, 0, low), (far_high, 0, low)],
    ]
    (early_own, early_sums), piece_c = tie(
        (
            fold(
                early,
                [own_turn, other_turn],
                [(0,) + q for q in quarters] + [(1, 0, cuts[2]), (1, depth, depth + cuts[2])],
                n_done=1,
            ),
            move(last_piece, dz=1),
        )
    )
    swapped_c = swap_cores(piece_c)
    last_turn = [(piece_c, 0, depth - cuts[2], cuts[2]), (swapped_c, 0, depth - cuts[2], depth + cuts[2])]
    by_x3, by_y3, swapped_a, swapped_b, swapped_c, (early_rows, (near_rows,)) = tie(
        (
            move(jnp.concatenate([far_high, by_y[2 * low - cut :]]), dx=1),
            move(jnp.concatenate([far_high, by_x[low : low + cut]]), dy=1),
            swapped_a,
            swapped_b,
            swapped_c,
            fold(
                early,
                [last_turn],
                [(0, cuts[2], depth), (0, depth + cuts[2], 2 * depth)],
                early_own,
                NEAR + [None],
                begun=early_sums,
            ),
        )
    )
    first = pieces[0].shape[0]
    part, swapped = piece_a[first:], swapped_a[first:]
    ordered_other = jnp.concatenate([jnp.where(core == 0, part, swapped), jnp.where(core == 0, swapped, part)])
    checks = jnp.concatenate([ordered, ordered_other], axis=1)
    widened = checks.astype(jnp.float32)
    squares = jnp.sum(widened * widened, axis=1)
    arrived = [piece_a, piece_b, piece_c, swapped_a, swapped_b, swapped_c]
    other_turn = [(v, 0, p.shape[0], q) for v, p, q in zip(arrived, pieces + pieces, places)]
    by_y4, by_x4, received_first, early_rows = tie(
        (
            move(by_x3[: low - cut], dy=1),
            move(by_y3[low - cut : low], dx=1),
            spread(early_rows[:1], 0),
            early_rows,
        )
    )
    late = [
        [(by_x, low, low), (by_x3, 0, low)],
        [(by_y, low, low), (by_y3, 0, low)],
        [(by_y3, low, cut), (by_x3, 2 * cut, low - cut), (by_y4, 0, low - cut), (by_x4, 0, cut)],
    ]
    received_near, received_far, (late_rows, (far_rows,)) = tie(
        (
            spread(early_rows[1:4], 0, NEAR[1:]),
            spread(early_rows[4:], 1),
            fold(
                late,
                [own_turn, other_turn],
                [(k,) + q for q in quarters for k in range(2)],
                (),
                NEAR[1:],
                [(early_rows[4], NEAR[0])],
            ),
        )
    )
    received_near = received_first + received_near
    products = jnp.concatenate([check(near_rows), check(far_rows)], axis=1)

    def quarter(value, dx, dy):
        size = n_tokens // 4
        return lax.dynamic_slice_in_dim(value, ((x ^ dx) * 2 + (y ^ dy)) * size, size, 0)

    def to_send(d):
        terms = three_terms(quarter(squares, *d))
        return jnp.concatenate([quarter(products, *d).astype(jnp.bfloat16), terms.astype(jnp.bfloat16)], axis=1)

    parts, received = tie(([move(to_send(d), *d) for d in NEAR[1:]], spread(late_rows[:2], 1, NEAR[1:])))
    received_far = received_far + received
    got = sum(v.astype(jnp.float32) for v in parts)
    sums = quarter(products, 0, 0) + got[:, : 8 * half]
    squares = quarter(squares, 0, 0) + jnp.sum(got[:, 8 * half :], axis=1)
    sums, squares = halve(sums, squares, z_hi, dz=2)
    result = (sums * lax.rsqrt(squares / D + EPS)[:, None] / math.sqrt(D)).astype(jnp.bfloat16)
    keep, give = split(result, 1, z_hi ^ core)
    got = swap_cores(give)
    both = jnp.concatenate([jnp.where(core == 0, keep, got), jnp.where(core == 0, got, keep)], axis=1)
    keep, give = split(both, 0, z_lo)
    keep, got, received = tie((keep, move(give, dz=1), spread(late_rows[2:], 1, NEAR[3:])))
    received_far = received_far + received
    placed = [((f,) + d, v) for f, values in enumerate((received_near, received_far)) for d, v in zip(NEAR, values)]
    served = whole_rows(placed, width)

    whole = jnp.stack([jnp.where(z_lo == 0, keep, got), jnp.where(z_lo == 0, got, keep)], axis=1)
    qkv = whole.reshape(own_count, 2, 2, 4, half).transpose(0, 1, 3, 2, 4).reshape(own_count, 16 * half)
    return (served[None], qkv)


def solution(mesh):
    placed = (P("slab", "panel"), P(), P("panel", "slab"), P(None, "slab"))
    small = mesh.shape["slab"] == 16 and mesh.shape["panel"] == 2
    return jax.shard_map(
        shards if small else general_shards,
        mesh=mesh,
        in_specs=placed,
        out_specs=(P("panel", "slab", None), P("slab", "panel")),
        check_vma=False,
    )
```

```python
import functools
import math

import jax
import jax.numpy as jnp
from jax import lax
from jax.experimental import pallas as pl
from jax.experimental.pallas import tpu as pltpu
from jax.sharding import PartitionSpec as P

D = 8192


EPS = 1e-05


def general_shards(weights, gain, rotation, tokens):
    width_rows = rotation.shape[0]
    gain_block = lax.dynamic_slice_in_dim(gain, lax.axis_index("panel") * width_rows, width_rows, 0)
    partial_value = jnp.dot(
        lax.all_gather(weights, "slab", axis=0, tiled=True),
        (rotation * gain_block[:, None]).astype(jnp.bfloat16),
        preferred_element_type=jnp.float32,
    )
    folded = lax.psum_scatter(partial_value, "panel", scatter_dimension=0, tiled=True)
    exported = folded.astype(jnp.bfloat16)
    product = lax.dot_general(
        tokens, exported, (((1,), (1,)), ((), ())), preferred_element_type=jnp.float32
    )
    widened = tokens.astype(jnp.float32)
    squares = jnp.sum(widened * widened, axis=1)
    whole, whole_squares = lax.psum((product, squares), "slab")
    own_count = tokens.shape[0] // lax.axis_size("slab")
    first_token = lax.axis_index("slab") * own_count
    total = lax.dynamic_slice_in_dim(whole, first_token, own_count, 0)
    square_sum = lax.dynamic_slice_in_dim(whole_squares, first_token, own_count, 0)
    meansq = square_sum / D
    qkv = (total * lax.rsqrt(meansq + EPS)[:, None] / math.sqrt(D)).astype(jnp.bfloat16)
    whole_rows = lax.all_to_all(exported, "slab", split_axis=0, concat_axis=1, tiled=True)
    return (whole_rows[None], qkv)


CHIPS = [(x, y, z) for z in range(4) for y in range(2) for x in range(2)]
NEAR = [(dx, dy) for dy in range(2) for dx in range(2)]


def slab_of(x, y, z):
    return z * 4 + y * 2 + x


def move(value, dx=0, dy=0, dz=0):
    pairs = [(slab_of(x, y, z), slab_of(x ^ dx, y ^ dy, z ^ dz)) for x, y, z in CHIPS]
    return lax.ppermute(value, "slab", pairs)


def swap_cores(value):
    return lax.ppermute(value, "panel", [(0, 1), (1, 0)])


def send_rows(value, f, dx, dy):
    pairs = []
    for x, y, z in CHIPS:
        for q in range(2):
            target = slab_of(q, x ^ dx, 2 * (z % 2) + (y ^ dy)) * 2 + ((z // 2) ^ f)
            pairs.append((slab_of(x, y, z) * 2 + q, target))
    return lax.ppermute(value, ("slab", "panel"), pairs)


def tie(values, *others):
    return lax.optimization_barrier((values, others))[0]


def fold_kernel(plan, turn_plan, steps, n_done, keys, ready_keys, n_begun, given, *refs):
    n, n_ready = len(keys), len(ready_keys)
    n_in = 1 + max(max(p[0] for p in plan), max(p[0] for turn in turn_plan for p in turn))
    ins, refs = refs[:n_in], refs[n_in:]
    begun, refs = refs[:n_begun], refs[n_begun:]
    before, ready, refs = refs[:given], refs[given : given + n_ready], refs[given + n_ready :]
    outs, more, (rows, held, sums, sems) = refs[:n], refs[n:-4], refs[-4:]
    n_rows, _ = rows.shape
    width = held.shape[2]
    size = n_rows // n
    slab = lax.axis_index("slab")
    x, y = slab % 2, (slab // 2) % 2

    def slot(key):
        return pl.ds(pl.multiple_of(((y + key[1]) % 2 * 2 + (x + key[0]) % 2) * size, 32), size)

    copies, index, loaded = [], 0, set()
    for k, begin, end in steps:
        group = []
        for p, first, count, place in turn_plan[k]:
            low, high = max(place, begin), min(place + count, end)
            if low < high:
                source = ins[p].at[pl.ds(first + low - place, high - low)]
                group.append(pltpu.make_async_copy(source, held.at[k, pl.ds(low, high - low)], sems.at[index]))
                index += 1
        if not any(low <= begin and end <= high for low, high in loaded):
            loaded.add((begin, end))
            loaded.update([(low, end) for low, high in loaded if high == begin])
            for p, first, count, place in plan:
                columns = pl.ds(begin, end - begin)
                source = ins[p].at[pl.ds(first, count), columns]
                group.append(pltpu.make_async_copy(source, rows.at[pl.ds(place, count), columns], sems.at[index]))
                index += 1
        copies.append(group)
    for group in copies[:2]:
        for copy in group:
            copy.start()
    shift = before[0].shape[1] if given else 0
    for value, key in zip(ready, ready_keys):
        more[0][slot(key), :] = value[...]
    last = {k: i for i, (k, _, _) in enumerate(steps)}
    started = set(range(n_begun))
    for i, (k, begin, end) in enumerate(steps):
        for copy in copies[i]:
            copy.wait()
        for copy in copies[i + 2] if i + 2 < len(steps) else []:
            copy.start()
        if given and not i:
            for out, value in zip(outs, before):
                out[:, :shift] = value[...]
        columns = slice(k * width, (k + 1) * width)
        value = jnp.dot(rows[:, begin:end], held[k, begin:end], preferred_element_type=jnp.float32)
        if k in started:
            value = value + (begun[k][...] if k < n_begun and (k, 0) not in started else sums[:, columns])
            started.add((k, 0))
        started.add(k)
        if i < last[k]:
            sums[:, columns] = value
            started.add((k, 0))
        elif k >= n_done:
            more[-1][...] = value
        else:
            value = value.astype(jnp.bfloat16)
            for j, out in enumerate(outs):
                out[:, shift + k * width : shift + (k + 1) * width] = value[j * size : (j + 1) * size]
    for out, key in zip(outs, keys):
        if key is not None:
            more[0][slot(key), :] = out[...]


def fold(blocks, turns, steps, before=(), keys=None, ready=(), begun=(), n_done=None):
    arrays, plan, turn_plan, place = [], [], [], 0

    def operand(value):
        for i, other in enumerate(arrays):
            if other is value:
                return i
        arrays.append(value)
        return len(arrays) - 1

    for block in blocks:
        for value, first, count in block:
            plan.append((operand(value), first, count, place))
            place += count
    for turn in turns:
        turn_plan.append([(operand(v), first, count, begin) for v, first, count, begin in turn])
    depth, width = blocks[0][0][0].shape[1], turns[0][0][0].shape[1]
    n, t = len(blocks), len(turns)
    n_done = t if n_done is None else n_done
    size, all_width = place // n, n_done * width + (before[0].shape[1] if before else 0)
    n_copies = len(steps) * (len(plan) + sum(len(turn) for turn in turn_plan))
    shapes = [jax.ShapeDtypeStruct((size, all_width), jnp.bfloat16)] * n
    if keys:
        shapes.append(jax.ShapeDtypeStruct((4 * size, all_width), jnp.bfloat16))
    if n_done < t:
        shapes.append(jax.ShapeDtypeStruct((place, width), jnp.float32))
    ready_values, ready_keys = [v for v, _ in ready], [k for _, k in ready]
    out = pl.pallas_call(
        functools.partial(
            fold_kernel, plan, turn_plan, steps, n_done, keys or [None] * n, ready_keys, len(begun), len(before)
        ),
        out_shape=shapes,
        in_specs=[pl.BlockSpec(memory_space=pltpu.HBM)] * len(arrays)
        + [pl.BlockSpec(memory_space=pltpu.VMEM)] * (len(begun) + len(before) + len(ready)),
        out_specs=[pl.BlockSpec(memory_space=pltpu.VMEM)] * len(shapes),
        scratch_shapes=[
            pltpu.VMEM((place, depth), jnp.bfloat16),
            pltpu.VMEM((t, depth, width), jnp.bfloat16),
            pltpu.VMEM((place, t * width), jnp.float32),
            pltpu.SemaphoreType.DMA((n_copies,)),
        ],
        compiler_params=pltpu.CompilerParams(vmem_limit_bytes=60 * 1024 * 1024),
        cost_estimate=pl.CostEstimate(flops=1024, bytes_accessed=1024, transcendentals=0),
    )(*arrays, *begun, *before, *ready_values)
    return out[:n], out[n:]


def place_kernel(plan, width, *refs):
    ins, out, sems = refs[:-2], refs[-2], refs[-1]
    slab, core = lax.axis_index("slab"), lax.axis_index("panel")
    x, y, z = slab % 2, (slab // 2) % 2, slab // 4
    copies = []
    for ref, (f, dx, dy) in zip(ins, plan):
        for j in range(2):
            z_source = (core + f) % 2 * 2 + (z // 2 + j) % 2
            source = z_source * 4 + (z + dy) % 2 * 2 + (y + dx) % 2
            target = out.at[:, pl.ds(pl.multiple_of(source * width, width), width)]
            copies.append(pltpu.make_async_copy(ref.at[:, pl.ds(j * width, width)], target, sems.at[len(copies)]))
    for copy in copies:
        copy.start()
    for copy in copies:
        copy.wait()


def whole_rows(pieces, width):
    plan = [key for key, _ in pieces]
    return pl.pallas_call(
        functools.partial(place_kernel, plan, width),
        out_shape=jax.ShapeDtypeStruct((pieces[0][1].shape[0], D), jnp.bfloat16),
        in_specs=[pl.BlockSpec(memory_space=pl.ANY)] * len(pieces),
        out_specs=pl.BlockSpec(memory_space=pltpu.VMEM),
        scratch_shapes=[pltpu.SemaphoreType.DMA((2 * len(plan),))],
        cost_estimate=pl.CostEstimate(flops=1024, bytes_accessed=1024, transcendentals=0),
    )(*[value for _, value in pieces])


def shards(weights, gain, rotation, tokens):
    slab, core = lax.axis_index("slab"), lax.axis_index("panel")
    x, y, z = slab % 2, (slab // 2) % 2, slab // 4
    z_hi, z_lo = z // 2, z % 2
    depth, width = rotation.shape
    half = weights.shape[0] // 2
    low = half // 2
    n_tokens = tokens.shape[0]
    own_count = n_tokens // 16

    def split(value, axis, bit):
        size = value.shape[axis] // 2
        return [lax.dynamic_slice_in_dim(value, b * size, size, axis) for b in (bit, 1 - bit)]

    mine, others = split(weights, 0, core)
    rows = jnp.concatenate([mine, swap_cores(others)], axis=1)

    ordered = tokens.reshape(2, 2, 2, 2, own_count, width).transpose(3, 2, 0, 1, 4, 5).reshape(n_tokens, width)
    part = split(ordered, 0, core)[0]

    gain_block = lax.dynamic_slice_in_dim(gain, core * depth, depth, 0)[:, None]
    cuts = [0, 7 * depth // 32, 17 * depth // 32, depth]
    first_piece = (rotation[: cuts[1]] * gain_block[: cuts[1]]).astype(jnp.bfloat16)
    rotation, gain_block = tie((rotation, gain_block), rows)
    turn = (rotation * gain_block).astype(jnp.bfloat16)
    pieces = [first_piece] + [turn[i:j] for i, j in zip(cuts[1:], cuts[2:])]

    def spread(values, f, keys=NEAR):
        return [send_rows(value, f, *key) for value, key in zip(values, keys)]

    def check(exported):
        return lax.dot_general(checks, exported, (((1,), (1,)), ((), ())), preferred_element_type=jnp.float32)

    def three_terms(values):
        terms = []
        for _ in range(3):
            terms.append(values.astype(jnp.bfloat16).astype(jnp.float32))
            values = values - terms[-1]
        return jnp.pad(jnp.stack(terms, axis=1), ((0, 0), (0, 125)))

    def halve(values, squares, bit, dx=0, dy=0, dz=0):
        keep, give = split(values, 0, bit)
        if dz:
            give = jnp.roll(give, give.shape[1] // 2, axis=1)
        keep_squares, give_squares = split(squares, 0, bit)
        got = move(jnp.concatenate([give, three_terms(give_squares)], axis=1).astype(jnp.bfloat16), dx, dy, dz)
        got = got.astype(jnp.float32)
        n = values.shape[1]
        return keep + got[:, :n], keep_squares + jnp.sum(got[:, n:], axis=1)

    near_x, near_y, far_low, piece_a, pieces = tie(
        (
            move(rows, dx=1),
            move(rows, dy=1),
            move(rows[:low], dz=2),
            move(jnp.concatenate([pieces[0], part]), dz=1),
            pieces,
        )
    )
    by_x, by_y, far_high, piece_b, turn_swapped, last_piece = tie(
        (
            move(jnp.concatenate([near_y[low:], far_low]), dx=1),
            move(jnp.concatenate([near_x[:low], far_low]), dy=1),
            move(rows[low:], dz=2),
            move(pieces[1], dz=1),
            swap_cores(turn),
            pieces[2],
        )
    )
    cut = 3 * low // 5
    own_turn = [(turn, 0, depth, 0), (turn_swapped, 0, depth, depth)]
    quarters = [(i * depth // 2, (i + 1) * depth // 2) for i in range(4)]
    swapped_a, swapped_b = swap_cores(piece_a), swap_cores(piece_b)
    places = cuts[:3] + [depth + cut for cut in cuts[:3]]
    other_turn = [(v, 0, p.shape[0], q) for v, p, q in zip([piece_a, piece_b, swapped_a, swapped_b], (pieces[:2]) * 2, [places[i] for i in (0, 1, 3, 4)])]
    early = [
        [(rows, 0, half)],
        [(near_x, 0, half)],
        [(near_y, 0, half)],
        [(by_y, 0, low), (by_x, 0, low)],
        [(far_low, 0, low), (far_high, 0, low)],
    ]
    (early_own, early_sums), piece_c = tie(
        (
            fold(
                early,
                [own_turn, other_turn],
                [(0,) + q for q in quarters] + [(1, 0, cuts[2]), (1, depth, depth + cuts[2])],
                n_done=1,
            ),
            move(last_piece, dz=1),
        )
    )
    swapped_c = swap_cores(piece_c)
    last_turn = [(piece_c, 0, depth - cuts[2], cuts[2]), (swapped_c, 0, depth - cuts[2], depth + cuts[2])]
    by_x3, by_y3, swapped_a, swapped_b, swapped_c, (early_rows, (near_rows,)) = tie(
        (
            move(jnp.concatenate([far_high, by_y[2 * low - cut :]]), dx=1),
            move(jnp.concatenate([far_high, by_x[low : low + cut]]), dy=1),
            swapped_a,
            swapped_b,
            swapped_c,
            fold(
                early,
                [last_turn],
                [(0, cuts[2], depth), (0, depth + cuts[2], 2 * depth)],
                early_own,
                NEAR + [None],
                begun=early_sums,
            ),
        )
    )
    first = pieces[0].shape[0]
    part, swapped = piece_a[first:], swapped_a[first:]
    ordered_other = jnp.concatenate([jnp.where(core == 0, part, swapped), jnp.where(core == 0, swapped, part)])
    checks = jnp.concatenate([ordered, ordered_other], axis=1)
    widened = checks.astype(jnp.float32)
    squares = jnp.sum(widened * widened, axis=1)
    arrived = [piece_a, piece_b, piece_c, swapped_a, swapped_b, swapped_c]
    other_turn = [(v, 0, p.shape[0], q) for v, p, q in zip(arrived, pieces + pieces, places)]
    by_y4, by_x4, received_first, early_rows = tie(
        (
            move(by_x3[: low - cut], dy=1),
            move(by_y3[low - cut : low], dx=1),
            spread(early_rows[:1], 0),
            early_rows,
        )
    )
    late = [
        [(by_x, low, low), (by_x3, 0, low)],
        [(by_y, low, low), (by_y3, 0, low)],
        [(by_y3, low, cut), (by_x3, 2 * cut, low - cut), (by_y4, 0, low - cut), (by_x4, 0, cut)],
    ]
    received_near, received_far, (late_rows, (far_rows,)) = tie(
        (
            spread(early_rows[1:4], 0, NEAR[1:]),
            spread(early_rows[4:], 1),
            fold(
                late,
                [own_turn, other_turn],
                [(k,) + q for q in quarters for k in range(2)],
                (),
                NEAR[1:],
                [(early_rows[4], NEAR[0])],
            ),
        )
    )
    received_near = received_first + received_near
    products = jnp.concatenate([check(near_rows), check(far_rows)], axis=1)

    def quarter(value, dx, dy):
        size = n_tokens // 4
        return lax.dynamic_slice_in_dim(value, ((x ^ dx) * 2 + (y ^ dy)) * size, size, 0)

    def to_send(d):
        terms = three_terms(quarter(squares, *d))
        return jnp.concatenate([quarter(products, *d).astype(jnp.bfloat16), terms.astype(jnp.bfloat16)], axis=1)

    parts, received = tie(([move(to_send(d), *d) for d in NEAR[1:]], spread(late_rows[:2], 1, NEAR[1:])))
    received_far = received_far + received
    got = sum(v.astype(jnp.float32) for v in parts)
    sums = quarter(products, 0, 0) + got[:, : 8 * half]
    squares = quarter(squares, 0, 0) + jnp.sum(got[:, 8 * half :], axis=1)
    sums, squares, received = tie(halve(sums, squares, z_hi, dz=2) + (spread(late_rows[2:], 1, NEAR[3:]),))
    received_far = received_far + received
    placed = [((f,) + d, v) for f, values in enumerate((received_near, received_far)) for d, v in zip(NEAR, values)]
    served = whole_rows(placed, width)

    result = (sums * lax.rsqrt(squares / D + EPS)[:, None] / math.sqrt(D)).astype(jnp.bfloat16)
    keep, give = split(result, 1, z_hi ^ core)
    got = swap_cores(give)
    both = jnp.concatenate([jnp.where(core == 0, keep, got), jnp.where(core == 0, got, keep)], axis=1)
    keep, give = split(both, 0, z_lo)
    got = move(give, dz=1)
    whole = jnp.stack([jnp.where(z_lo == 0, keep, got), jnp.where(z_lo == 0, got, keep)], axis=1)
    qkv = whole.reshape(own_count, 2, 2, 4, half).transpose(0, 1, 3, 2, 4).reshape(own_count, 16 * half)
    return (served[None], qkv)


def solution(mesh):
    placed = (P("slab", "panel"), P(), P("panel", "slab"), P(None, "slab"))
    small = mesh.shape["slab"] == 16 and mesh.shape["panel"] == 2
    return jax.shard_map(
        shards if small else general_shards,
        mesh=mesh,
        in_specs=placed,
        out_specs=(P("panel", "slab", None), P("slab", "panel")),
        check_vma=False,
    )
```
